512 devices in a mesh: replica: 32 (over x, y, core), expert: 16 (over z).
Axes of the slice: x: 4, y: 4, z: 16, core: 2. Of those that a mesh axis runs over, the one named last changes fastest.
Arguments:
- queries: bfloat16 [1024, 4096], P(('replica', 'expert'))
- fresh_key_value: bfloat16 [1024, 512], P(('replica', 'expert')), may hold values from -6 to 6
- resid: bfloat16 [1024, 4096], P(('replica', 'expert')), may hold values from -6 to 6
- norm_gain: float32 [4096], replicated, may hold values from 0.5 to 1.5
- res_cache: bfloat16 [512, 128, 512], P(('replica', 'expert'))
- res_len: int32 [512], P(('replica', 'expert')), may hold values from 2 to 128
- long_cache: bfloat16 [512, 256, 512], P(('replica', 'expert'))
- long_len: int32 [32, 16], P(None, 'expert'), may hold values from 2 to 256
- migrate_from: int32 [32, 16], P(None, 'expert'), may hold values from 0 to 31, as said below
- expert_ids: int32 [1024, 8], P(('replica', 'expert')), may hold values from 0 to 63, as said below
- gate_wts: float32 [1024, 8], P(('replica', 'expert')), may hold values from 0.05 to 0.4
- w_gate: bfloat16 [98304, 4096], P(('expert', 'replica')), may hold values from -0.09375 to 0.09375
- w_up: bfloat16 [98304, 4096], P(('expert', 'replica')), may hold values from -0.09375 to 0.09375
- w_down: bfloat16 [64, 1536, 4096], P('expert', None, 'replica'), may hold values from -0.15625 to 0.15625
Outputs:
- attn_out: bfloat16 [1024, 4096], P(('replica', 'expert'))
- layer_out: bfloat16 [1024, 4096], P(('replica', 'expert'))
The draws below stay inside these ranges and needn't reach their ends.
Inputs may be any that keep to these rules, and one draw needn't show every extreme that they name: For each expert index e, migrate_from[:, e] is a permutation of the replica indices. `expert_ids`: the 16 picks of one device name different experts; at most 2 of them lie in one expert index's experts (x // 4); in every draw, for some replica index, some expert index receives exactly 2 picks from every device of that replica index.
All inputs are finite; a program needn't handle non-finite values.
Results may differ from the reference program's by a relative error of at most 0.015.
Values may be sent and summed in bfloat16 or wider, within the bound.
No kernel may reach another device: no remote copies, remote signals or barrier semaphores. Data moves between devices by JAX's collectives and lax.ppermute only.
A program may use at most 64 MiB of HBM per device.

```python
import math
import jax
import jax.numpy as jnp
from jax import lax

D = 4096
QUERY_HEADS = 32
KEY_VALUE_HEADS = 2
HEAD_SIZE = 128
TOP = 8
EXP_DEV = 4
FFW = 1536
RESIDENT_SLOTS = 128
LONG_SLOTS = 256
EXPERTS = 64
CAP = 2
ROW_TOTAL = 1024
N_REPLICA = 32
N_EXPERT = 16
DEVICES = 512


def migration(key):
    key_rows = jax.random.split(jax.random.fold_in(key, 101), N_EXPERT)
    columns = jax.vmap(lambda single: jax.random.permutation(single, N_REPLICA))(key_rows)
    return columns.T.astype(jnp.int32)


def draw_queries(key, part):
    key = jax.random.fold_in(key, 3)
    value_rows = jax.random.normal(key, (2 * DEVICES, QUERY_HEADS * HEAD_SIZE))
    return value_rows.astype(jnp.bfloat16)


def draw_res_cache(key, part):
    key = jax.random.fold_in(key, 1)
    cache_store = jax.random.normal(key, (DEVICES, RESIDENT_SLOTS, 2 * KEY_VALUE_HEADS * HEAD_SIZE))
    return cache_store.astype(jnp.bfloat16)


def draw_long_cache(key, part):
    key = jax.random.fold_in(key, 2)
    cache_store = jax.random.normal(key, (DEVICES, LONG_SLOTS, 2 * KEY_VALUE_HEADS * HEAD_SIZE))
    return cache_store.astype(jnp.bfloat16)


def draw_migrate_from(key, part):
    shared = migration(key)
    return shared


def draw_res_len(key, part):
    key = jax.random.fold_in(key, 5)
    lengths = jax.random.randint(key, (DEVICES,), 2, RESIDENT_SLOTS + 1)
    spot = jax.random.randint(jax.random.fold_in(key, 1), (), 0, DEVICES)
    return jnp.where(jnp.arange(DEVICES) == spot, RESIDENT_SLOTS, lengths).astype(jnp.int32)


def draw_long_len(key, part):
    key = jax.random.fold_in(key, 6)
    lengths = jax.random.randint(key, (N_REPLICA * N_EXPERT,), 2, LONG_SLOTS + 1)
    spot = jax.random.randint(jax.random.fold_in(key, 1), (), 0, N_REPLICA * N_EXPERT)
    lengths = jnp.where(jnp.arange(N_REPLICA * N_EXPERT) == spot, LONG_SLOTS, lengths)
    return lengths.reshape(N_REPLICA, N_EXPERT).astype(jnp.int32)


def draw_expert_ids(key, part):
    key = jax.random.fold_in(key, 7)
    slots = N_EXPERT * CAP
    busy = jax.random.randint(jax.random.fold_in(key, 1), (N_REPLICA,), 0, N_EXPERT)
    busy = jnp.repeat(busy, N_EXPERT)
    scores = jax.vmap(lambda single: jax.random.permutation(single, slots))(jax.random.split(jax.random.fold_in(key, 2), DEVICES))
    owner_of = jnp.arange(slots) // CAP
    scores = scores + jnp.where(owner_of[None, :] == busy[:, None], -slots, 0)
    chosen = jnp.argsort(scores, axis=1)[:, :2 * TOP]
    mixing = jax.vmap(lambda single: jax.random.permutation(single, 2 * TOP))(jax.random.split(jax.random.fold_in(key, 3), DEVICES))
    chosen = jnp.take_along_axis(chosen, mixing, axis=1)
    offset = jax.random.randint(jax.random.fold_in(key, 4), (DEVICES, N_EXPERT), 0, EXP_DEV)
    owner = chosen // CAP
    local = (chosen % CAP + jnp.take_along_axis(offset, owner, axis=1)) % EXP_DEV
    return (owner * EXP_DEV + local).reshape(2 * DEVICES, TOP).astype(jnp.int32)


def level_of(own_key, extent, cuts, least, largest):
    def one(axis_at, blocks):
        draws = jax.random.uniform(jax.random.fold_in(jax.random.fold_in(own_key, 6), axis_at), (blocks,), jnp.float32, least / len(cuts), largest / len(cuts))
        return jnp.repeat(jnp.exp(draws), extent[axis_at] // blocks).reshape((-1,) + (1,) * (len(extent) - axis_at - 1))

    loudness = one(*cuts[0])
    for cut in cuts[1:]:
        loudness = loudness * one(*cut)
    return loudness


def noise(stream_key, shape, scale, bound, pieces=(), kind=jnp.bfloat16):
    entries = scale * jax.random.normal(stream_key, shape, jnp.float32)
    if pieces:
        entries = entries * level_of(stream_key, shape, pieces, -0.22, 0.18)
    return jnp.clip(entries, -bound, bound).astype(kind)


def setup_inputs(seed: int = 0) -> dict:
    seeds = jax.random.split(jax.random.key(seed), 15)
    queries = draw_queries(jax.random.fold_in(seeds[14], 71), 0)
    fresh_key_value = noise(seeds[1], (ROW_TOTAL, 2 * KEY_VALUE_HEADS * HEAD_SIZE), 1.0, 6.0, ((0, 512),))
    resid = noise(seeds[2], (ROW_TOTAL, D), 1.0, 6.0, ((0, 512),))
    norm_gain = jnp.clip(1.0 + 0.1 * jax.random.normal(seeds[3], (D,), jnp.float32), 0.5, 1.5)
    res_cache = draw_res_cache(jax.random.fold_in(seeds[14], 71), 0)
    res_len = draw_res_len(jax.random.fold_in(seeds[14], 71), 0)
    long_cache = draw_long_cache(jax.random.fold_in(seeds[14], 71), 0)
    long_len = draw_long_len(jax.random.fold_in(seeds[14], 71), 0)
    migrate_from = draw_migrate_from(jax.random.fold_in(seeds[14], 71), 0)
    expert_ids = draw_expert_ids(jax.random.fold_in(seeds[14], 71), 0)
    gate_wts = jnp.clip(0.05 + 0.35 * jax.random.uniform(seeds[10], (ROW_TOTAL, TOP), jnp.float32) ** level_of(seeds[10], (ROW_TOTAL, TOP), ((0, 512),), -0.2, 0.2), 0.05, 0.4)
    w_gate = noise(seeds[11], (EXPERTS * FFW, D), D ** -0.5, 0.09375, ((0, 512),))
    w_up = noise(seeds[12], (EXPERTS * FFW, D), D ** -0.5, 0.09375, ((0, 512),))
    w_down = noise(seeds[13], (EXPERTS, FFW, D), FFW ** -0.5, 0.15625, ((0, 16), (2, 32)))
    return {"queries": queries, "fresh_key_value": fresh_key_value, "resid": resid, "norm_gain": norm_gain, "res_cache": res_cache, "res_len": res_len, "long_cache": long_cache, "long_len": long_len, "migrate_from": migrate_from, "expert_ids": expert_ids, "gate_wts": gate_wts, "w_gate": w_gate, "w_up": w_up, "w_down": w_down}


def attend(query_vector, cache_store, length, fresh):
    head_group = QUERY_HEADS // KEY_VALUE_HEADS
    row_list = jnp.concatenate([cache_store, fresh[None, :]], axis=0).astype(jnp.float32)
    count_number = row_list.shape[0]
    key_rows = row_list[:, :KEY_VALUE_HEADS * HEAD_SIZE].reshape(count_number, KEY_VALUE_HEADS, HEAD_SIZE)
    value_rows = row_list[:, KEY_VALUE_HEADS * HEAD_SIZE:].reshape(count_number, KEY_VALUE_HEADS, HEAD_SIZE)
    head_list = query_vector.astype(jnp.float32).reshape(KEY_VALUE_HEADS, head_group, HEAD_SIZE)
    scores = jnp.einsum('kgd,nkd->kgn', head_list, key_rows) * (1.0 / math.sqrt(HEAD_SIZE))
    place = jnp.arange(count_number)
    valid = (place < length) | (place == count_number - 1)
    scores = jnp.where(valid[None, None, :], scores, -1e+30)
    peak = lax.optimization_barrier(jnp.max(scores, axis=-1, keepdims=True))
    weights = jnp.where(valid[None, None, :], jnp.exp(scores - peak), 0.0).astype(jnp.bfloat16)
    weights = lax.optimization_barrier(weights).astype(jnp.float32)
    total = lax.optimization_barrier(jnp.sum(weights, axis=-1))
    summed = jnp.einsum('kgn,nkd->kgd', weights, value_rows)
    return (summed / total[..., None]).reshape(QUERY_HEADS * HEAD_SIZE).astype(jnp.bfloat16)

def expert_mixture(normed, expert_ids, gate_wts, w_gate, w_up, w_down):
    gate_all = w_gate.reshape(EXPERTS, FFW, D)
    up_all = w_up.reshape(EXPERTS, FFW, D)
    flat = expert_ids.reshape(-1).astype(jnp.int32)
    order = jnp.argsort(flat, stable=True).astype(jnp.int32)
    ranked = flat[order]
    bounds = jnp.searchsorted(ranked, jnp.arange(EXPERTS + 1, dtype=jnp.int32), side='left').astype(jnp.int32)
    weights_flat = gate_wts.reshape(-1)
    block_tile = 64
    total_picks = flat.shape[0]

    def per_expert(which, mixture):
        first = bounds[which]
        last = bounds[which + 1]
        gate_mat = gate_all[which]
        up_mat = up_all[which]
        down_mat = w_down[which]

        def going(state):
            return state[0] < last

        def advance(state):
            begin, acc = state
            place = begin + jnp.arange(block_tile, dtype=jnp.int32)
            live = place < last
            picked = order[jnp.minimum(place, total_picks - 1)]
            row_list = (picked // TOP).astype(jnp.int32)
            inputs = normed[row_list]
            gate = jnp.dot(inputs, gate_mat.T, preferred_element_type=jnp.float32)
            up = jnp.dot(inputs, up_mat.T, preferred_element_type=jnp.float32)
            act = (jax.nn.silu(gate) * up).astype(jnp.bfloat16)
            produced = jnp.dot(act, down_mat, preferred_element_type=jnp.float32).astype(jnp.bfloat16)
            scale = jnp.where(live, weights_flat[picked], 0.0)
            acc = acc.at[row_list].add(scale[:, None] * produced.astype(jnp.float32))
            return (begin + block_tile, acc)
        return lax.while_loop(going, advance, (first, mixture))[1]
    start = jnp.zeros((normed.shape[0], D), jnp.float32)
    return lax.fori_loop(0, EXPERTS, per_expert, start)

def reference(queries, fresh_key_value, resid, norm_gain, res_cache, res_len, long_cache, long_len, migrate_from, expert_ids, gate_wts, w_gate, w_up, w_down):

    def device_rows(index):
        replica = index // N_EXPERT
        column = index % N_EXPERT
        own = attend(queries[2 * index], res_cache[index], res_len[index], fresh_key_value[2 * index])
        root = migrate_from[replica, column]
        holder = root * N_EXPERT + column
        guest = attend(queries[2 * index + 1], long_cache[holder], long_len[root, column], fresh_key_value[2 * index + 1])
        return jnp.stack([own, guest])
    attn_out = lax.map(device_rows, jnp.arange(DEVICES, dtype=jnp.int32)).reshape(2 * DEVICES, QUERY_HEADS * HEAD_SIZE)
    stream = resid.astype(jnp.float32) + attn_out.astype(jnp.float32)
    normed = (stream * lax.rsqrt(lax.optimization_barrier(jnp.mean(stream * stream, axis=-1, keepdims=True)) + 1e-06) * norm_gain).astype(jnp.bfloat16)
    mixture = expert_mixture(normed, expert_ids, gate_wts, w_gate, w_up, w_down)
    layer_out = (stream + mixture).astype(jnp.bfloat16)
    return (attn_out, layer_out)
```

```python
import functools
import math

import jax
import jax.numpy as jnp
from jax import lax
from jax.experimental import pallas as pl
from jax.experimental.pallas import tpu as pltpu
from jax.sharding import Mesh
from jax.sharding import PartitionSpec as P

HEADS = 32
GROUP = 16
HEAD = 128
D = 4096
FFW = 1536
LOCAL = 4
UNITS = 192
PLANE = ("x", "y", "c")
XY = ("x", "y")
ALL = ("x", "y", "c", "z")
VMEM = pl.BlockSpec(memory_space=pltpu.VMEM)
SMEM = pl.BlockSpec(memory_space=pltpu.SMEM)


def params(mib):
    return pltpu.CompilerParams(vmem_limit_bytes=mib << 20)


def attend(q, cache_ref, fresh, length):
    slots = cache_ref.shape[0]
    fresh = fresh.astype(jnp.float32)
    outs = []
    for g in range(2):
        qg = q[g * GROUP : (g + 1) * GROUP]
        keys = cache_ref[:, g * HEAD : (g + 1) * HEAD]
        values = cache_ref[:, (2 + g) * HEAD : (3 + g) * HEAD]
        scale = 1.0 / math.sqrt(HEAD)
        scores = lax.dot_general(
            qg, keys, (((1,), (1,)), ((), ())), preferred_element_type=jnp.float32
        )
        scores = scores * scale
        live = lax.broadcasted_iota(jnp.int32, (GROUP, slots), 1) < length
        scores = jnp.where(live, scores, -1e30)
        last = (
            jnp.sum(qg.astype(jnp.float32) * fresh[g : g + 1], axis=1, keepdims=True)
            * scale
        )
        peak = jnp.maximum(jnp.max(scores, axis=1, keepdims=True), last)
        weights = jnp.where(live, jnp.exp(scores - peak), 0.0).astype(jnp.bfloat16)
        end = jnp.exp(last - peak).astype(jnp.bfloat16).astype(jnp.float32)
        total = jnp.sum(weights.astype(jnp.float32), axis=1, keepdims=True) + end
        summed = jnp.dot(weights, values, preferred_element_type=jnp.float32)
        summed = summed + end * fresh[2 + g : 3 + g]
        outs.append(summed / total)
    return jnp.concatenate(outs, axis=0)


def resident_kernel(len_ref, q_ref, kv_ref, cache_ref, out_ref):
    out = attend(q_ref[...], cache_ref, kv_ref[...], len_ref[0])
    out_ref[...] = out.astype(jnp.bfloat16)


def guest_kernel(me_ref, from_ref, len_ref, asked_ref, cache_ref, out_ref):
    me = me_ref[0]

    def look(i, found):
        return jnp.where(from_ref[i] == me, i, found)

    target = lax.fori_loop(0, from_ref.shape[0], look, 0)
    asked = asked_ref[target]
    out = attend(asked[:32], cache_ref, asked[32:48][:4], len_ref[me])
    out = out.astype(jnp.bfloat16)
    for r in range(out_ref.shape[0]):
        out_ref[r] = out


def token_kernel(
    me_ref, from_ref, own_ref, back_ref, resid_ref, gain_ref, meta_ref, attn_ref, stream_ref, out_ref
):
    root = from_ref[me_ref[0]]
    rows = (own_ref[...], back_ref[root])
    for r in range(2):
        attn_ref[r] = rows[r]
        stream = resid_ref[r].astype(jnp.float32) + rows[r].astype(jnp.float32)
        stream_ref[r] = stream
        square = jnp.sum(jnp.sum(stream * stream, axis=1, keepdims=True), axis=0, keepdims=True)
        normed = (stream * lax.rsqrt(square / D + 1e-06) * gain_ref[...]).astype(jnp.bfloat16)
        for e in range(out_ref.shape[0]):
            out_ref[e, r * 32 : (r + 1) * 32] = normed
    for e in range(out_ref.shape[0]):
        out_ref[e, 64:80] = meta_ref[e]


def select_kernel(rows_ref, meta_ref, out_ref):
    meta = meta_ref[...]
    first = rows_ref[:, :D].astype(jnp.float32)
    second = rows_ref[:, D:].astype(jnp.float32)
    for x in range(LOCAL):
        pick = meta[:, 16 + x : 17 + x].astype(jnp.float32) > 0.5
        row = jnp.where(pick, second, first).astype(jnp.bfloat16)
        for y in range(4):
            out_ref[x * 4 + y, :, :D] = row
            out_ref[x * 4 + y, :, D:] = meta


def up_kernel(core_ref, rows_ref, ga_ref, ua_ref, gb_ref, ub_ref, out_ref, gate_ref):
    rows = rows_ref[:, :D]
    dims = (((1,), (1,)), ((), ()))

    def act(g_ref, u_ref):
        gate = lax.dot_general(rows, g_ref[...], dims, preferred_element_type=jnp.float32)
        up = lax.dot_general(rows, u_ref[...], dims, preferred_element_type=jnp.float32)
        return gate * (1.0 / (1.0 + jnp.exp(-gate))) * up

    own = act(ga_ref, ua_ref)
    other = act(gb_ref, ub_ref)
    even = core_ref[0] == 0
    both = jnp.where(
        even,
        jnp.concatenate([own, other], axis=1),
        jnp.concatenate([other, own], axis=1),
    ).astype(jnp.bfloat16)
    n = rows.shape[0]
    to = lax.broadcasted_iota(jnp.int32, (n, n), 0)
    at = lax.broadcasted_iota(jnp.int32, (n, n), 1)
    swap = jnp.where((to % 16) * 16 + to // 16 == at, 1.0, 0.0).astype(jnp.bfloat16)
    both = jnp.dot(swap, both, preferred_element_type=jnp.float32).astype(jnp.bfloat16)
    gate_ref[...] = jnp.dot(swap, rows_ref[:, D:], preferred_element_type=jnp.float32)
    for p in range(out_ref.shape[0]):
        out_ref[p] = both


def down_kernel(act_ref, wa_ref, wb_ref, gate_ref, out_ref):
    gates = gate_ref[...]
    width = 2 * UNITS
    sums = [0.0, 0.0]
    for x in range(LOCAL):
        total = 0.0
        for y in range(4):
            block = pl.ds(y * width, width)
            w = jnp.concatenate([wa_ref[x, block], wb_ref[x, block]], axis=1)
            total += jnp.dot(act_ref[x * 4 + y], w, preferred_element_type=jnp.float32)
        for r in range(2):
            j = r * LOCAL + x
            weight = gates[:, j : j + 1] + gates[:, 8 + j : 9 + j]
            sums[r] += weight * total
    for r in range(2):
        part = sums[r].astype(jnp.bfloat16)
        for z in range(16):
            out_ref[z, r] = part[z * 16 : (z + 1) * 16]


def exchange(a, axes):
    return lax.all_to_all(a, axes, split_axis=0, concat_axis=0, tiled=True)


def pick_table(expert_ids, gate_wts, owners):
    wanted = jnp.arange(owners * LOCAL).reshape(owners, 1, LOCAL, 1)
    hit = expert_ids[None, :, None, :] == wanted
    gates = jnp.sum(jnp.where(hit, gate_wts[None, :, None, :], 0.0), axis=-1)
    high = gates.astype(jnp.bfloat16)
    rest = (gates - high.astype(jnp.float32)).astype(jnp.bfloat16)
    second = jnp.any(hit[:, 1], axis=-1).astype(jnp.bfloat16)
    line = jnp.concatenate([high.reshape(owners, 8), rest.reshape(owners, 8), second], axis=1)
    return jnp.pad(line[:, None, :], ((0, 0), (0, 15), (0, 108)))


def on_device(
    queries,
    fresh_key_value,
    resid,
    norm_gain,
    res_cache,
    res_len,
    long_cache,
    long_len,
    migrate_from,
    expert_ids,
    gate_wts,
    w_gate,
    w_up,
    w_down,
):
    bf16, f32 = jnp.bfloat16, jnp.float32
    core = lax.axis_index("c").reshape(1)
    me = lax.axis_index(PLANE).reshape(1)
    owners = 16
    swap = lambda a: lax.ppermute(a, "c", [(0, 1), (1, 0)])

    q = queries.reshape(2, HEADS, HEAD)
    kv = fresh_key_value.reshape(2, 4, HEAD)
    ask = jnp.concatenate([q[1], jnp.pad(kv[1], ((0, 12), (0, 0)))], axis=0)
    asked = exchange(jnp.broadcast_to(ask[None], (32, 48, HEAD)), PLANE)

    gate_b, up_b, down_b = swap(w_gate), swap(w_up), swap(w_down)
    own = pl.pallas_call(
        resident_kernel,
        out_shape=jax.ShapeDtypeStruct((HEADS, HEAD), bf16),
        in_specs=[SMEM, VMEM, VMEM, VMEM],
        out_specs=VMEM,
        name="resident_attention",
    )(res_len, q[0], kv[0], res_cache[0])
    source = migrate_from.reshape(32)
    guest = pl.pallas_call(
        guest_kernel,
        out_shape=jax.ShapeDtypeStruct((32, HEADS, HEAD), bf16),
        in_specs=[SMEM, SMEM, SMEM, VMEM, VMEM],
        out_specs=VMEM,
        name="guest_attention",
    )(me, source, long_len.reshape(32), asked, long_cache[0])
    back = exchange(guest, PLANE)
    meta = pick_table(expert_ids, gate_wts, owners)
    attn, stream, tokens = pl.pallas_call(
        token_kernel,
        out_shape=(
            jax.ShapeDtypeStruct((2, HEADS, HEAD), bf16),
            jax.ShapeDtypeStruct((2, HEADS, HEAD), f32),
            jax.ShapeDtypeStruct((owners, 80, HEAD), bf16),
        ),
        in_specs=[SMEM, SMEM] + [VMEM] * 5,
        out_specs=(VMEM, VMEM, VMEM),
        name="tokens",
    )(me, source, own, back, resid.reshape(2, HEADS, HEAD), norm_gain.reshape(HEADS, HEAD), meta)
    arrived = exchange(tokens, "z")
    rows = arrived[:, :64].reshape(owners, 2 * D)
    chosen = pl.pallas_call(
        select_kernel,
        out_shape=jax.ShapeDtypeStruct((16, owners, D + HEAD), bf16),
        in_specs=[VMEM, VMEM],
        out_specs=VMEM,
        compiler_params=params(32),
        name="select_rows",
    )(rows, arrived[:, 64])
    chosen = exchange(chosen, XY).reshape(16 * owners, D + HEAD)
    hidden, gates = pl.pallas_call(
        up_kernel,
        out_shape=(
            jax.ShapeDtypeStruct((16, 256, 2 * UNITS), bf16),
            jax.ShapeDtypeStruct((256, HEAD), f32),
        ),
        in_specs=[SMEM] + [VMEM] * 5,
        out_specs=(VMEM, VMEM),
        compiler_params=params(40),
        name="gate_up",
    )(core, chosen, w_gate, w_up, gate_b, up_b)
    hidden = exchange(hidden, XY)
    partial = pl.pallas_call(
        down_kernel,
        out_shape=jax.ShapeDtypeStruct((owners, 2, 16, 2 * HEAD), bf16),
        in_specs=[VMEM] * 4,
        out_specs=VMEM,
        compiler_params=params(40),
        name="down",
    )(hidden, w_down, down_b, gates)
    landed = exchange(partial, "z")
    summed = jnp.sum(landed.astype(f32), axis=0).transpose(1, 0, 2)
    mixture = exchange(summed, XY).reshape(16, 2, 2, HEAD)
    mixture = jnp.where(core[0] == 0, mixture, mixture[:, :, ::-1])
    mixture = mixture.transpose(1, 0, 2, 3).reshape(2, D)
    layer_out = (stream.reshape(2, D) + mixture).astype(bf16)
    return attn.reshape(2, D), layer_out


def solution(mesh):
    fine = Mesh(mesh.devices.reshape(4, 4, 2, 16), ALL)
    rows, experts = P(ALL, None), P(("z", "x", "y", "c"), None)
    cache = P(ALL, None, None)
    placed = (
        rows,
        rows,
        rows,
        P(),
        cache,
        P(ALL),
        cache,
        P(None, "z"),
        P(None, "z"),
        rows,
        rows,
        experts,
        experts,
        P("z", None, PLANE),
    )
    return jax.shard_map(
        on_device, mesh=fine, in_specs=placed, out_specs=(rows, rows), check_vma=False
    )
```

```python
import functools
import math

import jax
import jax.numpy as jnp
from jax import lax
from jax.experimental import pallas as pl
from jax.experimental.pallas import tpu as pltpu
from jax.sharding import Mesh
from jax.sharding import PartitionSpec as P

HEADS = 32
GROUP = 16
HEAD = 128
D = 4096
FFW = 1536
LOCAL = 4
UNITS = 192
X = ("xh", "xl")
Y = ("yh", "yl")
XY = X + Y
PLANE = XY + ("c",)
Z = ("zh", "zl")
ALL = PLANE + Z
VMEM = pl.BlockSpec(memory_space=pltpu.VMEM)
SMEM = pl.BlockSpec(memory_space=pltpu.SMEM)
HBM = pl.BlockSpec(memory_space=pltpu.HBM)


def params(mib):
    return pltpu.CompilerParams(vmem_limit_bytes=mib << 20)


def attend(q, cache_ref, fresh, length):
    slots = cache_ref.shape[0]
    fresh = fresh.astype(jnp.float32)
    outs = []
    for g in range(2):
        qg = q[g * GROUP : (g + 1) * GROUP]
        keys = cache_ref[:, g * HEAD : (g + 1) * HEAD]
        values = cache_ref[:, (2 + g) * HEAD : (3 + g) * HEAD]
        scale = 1.0 / math.sqrt(HEAD)
        scores = lax.dot_general(
            qg, keys, (((1,), (1,)), ((), ())), preferred_element_type=jnp.float32
        )
        scores = scores * scale
        live = lax.broadcasted_iota(jnp.int32, (GROUP, slots), 1) < length
        scores = jnp.where(live, scores, -1e30)
        last = (
            jnp.sum(qg.astype(jnp.float32) * fresh[g : g + 1], axis=1, keepdims=True)
            * scale
        )
        peak = jnp.maximum(jnp.max(scores, axis=1, keepdims=True), last)
        weights = jnp.where(live, jnp.exp(scores - peak), 0.0).astype(jnp.bfloat16)
        end = jnp.exp(last - peak).astype(jnp.bfloat16).astype(jnp.float32)
        total = jnp.sum(weights.astype(jnp.float32), axis=1, keepdims=True) + end
        summed = jnp.dot(weights, values, preferred_element_type=jnp.float32)
        summed = summed + end * fresh[2 + g : 3 + g]
        outs.append(summed / total)
    return jnp.concatenate(outs, axis=0)


def ask_kernel(q_ref, kv_ref, ask_ref, own_ref, line_ref):
    q = q_ref[...].astype(jnp.float32)
    kv = kv_ref[...].astype(jnp.float32)
    line_ref[...] = jnp.zeros(line_ref.shape, jnp.float32)
    for r in range(2):
        for h in range(HEADS):
            line_ref[r, h : h + 1] = q[r : r + 1, h * HEAD : (h + 1) * HEAD]
        for h in range(4):
            line_ref[r, 32 + h : 33 + h] = kv[r : r + 1, h * HEAD : (h + 1) * HEAD]
    own_ref[...] = line_ref[0].astype(jnp.bfloat16)
    ask = line_ref[1].astype(jnp.bfloat16)
    for p in range(ask_ref.shape[0]):
        ask_ref[p] = ask


def resident_kernel(len_ref, own_ref, cache_ref, out_ref):
    own = own_ref[...]
    out = attend(own[:32], cache_ref, own[32:48][:4], len_ref[0])
    out_ref[...] = out.astype(jnp.bfloat16)


def guest_kernel(me_ref, from_ref, len_ref, asked_ref, cache_ref, out_ref):
    me = me_ref[0]

    def look(i, found):
        return jnp.where(from_ref[i] == me, i, found)

    target = lax.fori_loop(0, from_ref.shape[0], look, 0)
    asked = asked_ref[target]
    out = attend(asked[:32], cache_ref, asked[32:48][:4], len_ref[me])
    out = out.astype(jnp.bfloat16)
    for r in range(out_ref.shape[0]):
        out_ref[r] = out


def token_kernel(
    me_ref, from_ref, own_ref, back_ref, resid_ref, gain_ref, meta_ref, attn_ref, stream_ref, out_ref
):
    root = from_ref[me_ref[0]]
    rows = (own_ref[...], back_ref[root])
    for r in range(2):
        attn_ref[r] = rows[r]
        stream = resid_ref[r].astype(jnp.float32) + rows[r].astype(jnp.float32)
        stream_ref[r] = stream
        square = jnp.sum(jnp.sum(stream * stream, axis=1, keepdims=True), axis=0, keepdims=True)
        normed = (stream * lax.rsqrt(square / D + 1e-06) * gain_ref[...]).astype(jnp.bfloat16)
        for e in range(out_ref.shape[0]):
            out_ref[e, r * 32 : (r + 1) * 32] = normed
    for e in range(out_ref.shape[0]):
        out_ref[e, 64:80] = meta_ref[...]


def select_kernel(expert_ref, rows_ref, meta_ref, out_ref):
    meta = meta_ref[...].astype(jnp.float32)
    mine = lax.broadcasted_iota(jnp.int32, meta.shape, 1) == expert_ref[0]
    meta = jnp.sum(jnp.where(mine, meta, 0.0), axis=1)
    line = meta.astype(jnp.bfloat16)
    first = rows_ref[:, :D].astype(jnp.float32)
    second = rows_ref[:, D:].astype(jnp.float32)
    for x in range(LOCAL):
        pick = meta[:, 16 + x : 17 + x] > 0.5
        row = jnp.where(pick, second, first).astype(jnp.bfloat16)
        for y in range(4):
            out_ref[x * 4 + y, :, :D] = row
            out_ref[x * 4 + y, :, D:] = line


def up_kernel(
    core_ref, rows_ref, ga_ref, ua_ref, gb_ref, ub_ref, out_ref, gate_ref, held_ref, sems
):
    copies = [
        pltpu.make_async_copy(w_ref, held_ref.at[pl.ds(i * UNITS, UNITS)], sems.at[i])
        for i, w_ref in enumerate((ga_ref, ua_ref, gb_ref, ub_ref))
    ]
    for copy in copies:
        copy.start()
    for copy in copies:
        copy.wait()
    dims = (((1,), (1,)), ((), ()))
    total = lax.dot_general(
        rows_ref[:, :D], held_ref[...], dims, preferred_element_type=jnp.float32
    )
    parts = [total[:, i * UNITS : (i + 1) * UNITS] for i in range(4)]
    acts = [
        gate * (1.0 / (1.0 + jnp.exp(-gate))) * up
        for gate, up in (parts[:2], parts[2:])
    ]
    both = jnp.where(
        core_ref[0] == 0,
        jnp.concatenate(acts, axis=1),
        jnp.concatenate(acts[::-1], axis=1),
    ).astype(jnp.bfloat16)
    for x in range(4):
        for y in range(4):
            there = slice((x * 4 + y) * 16, (x * 4 + y + 1) * 16)
            here = slice((x // 2 * 2 + y // 2) * 16, (x // 2 * 2 + y // 2 + 1) * 16)
            gate_ref[x % 2 * 2 + y % 2, here] = rows_ref[there, D:]
            for to_x in (x % 2, x % 2 + 2):
                for to_y in (y % 2, y % 2 + 2):
                    out_ref[to_x * 4 + to_y, here] = both[there]


def down_kernel(place_ref, act_ref, gate_ref, *refs):
    w_refs, (out_ref, held_ref, sems) = refs[:10], refs[10:]
    copies = []
    for x in range(LOCAL):
        sources = []
        for c in range(2):
            own, by_x, by_both, *by_y = w_refs[5 * c : 5 * c + 5]
            sources += [own.at[x], by_x.at[x], by_y[x // 2].at[x % 2], by_both.at[x]]
        copies.append(
            [
                pltpu.make_async_copy(source, held_ref.at[x, i], sems.at[x, i])
                for i, source in enumerate(sources)
            ]
        )
        for copy in copies[-1]:
            copy.start()
    n = act_ref.shape[1]
    row = lax.broadcasted_iota(jnp.int32, (2 * n, n), 0)
    slot = lax.broadcasted_iota(jnp.int32, (2 * n, n), 1)
    twice = jnp.where(row // 2 == slot, 1.0, 0.0).astype(jnp.bfloat16)
    gates = gate_ref[place_ref[0] * 2 + place_ref[1]]
    gates = jnp.dot(twice, gates, preferred_element_type=jnp.float32)
    lane = lax.broadcasted_iota(jnp.int32, gates.shape, 1)
    second = lax.broadcasted_iota(jnp.int32, gates.shape, 0) % 2
    sums = [0.0] * 4
    for x in range(LOCAL):
        act = jnp.concatenate([act_ref[x * 4 + y] for y in range(4)], axis=1)
        act = jnp.dot(twice, act, preferred_element_type=jnp.float32).astype(jnp.bfloat16)
        at = second * LOCAL + x
        weight = jnp.sum(
            jnp.where((lane == at) | (lane == at + 8), gates, 0.0), axis=1, keepdims=True
        )
        for copy in copies[x]:
            copy.wait()
        for b in range(4):
            w = jnp.concatenate([held_ref[x, 2 * b], held_ref[x, 2 * b + 1]], axis=1)
            sums[b] += weight * jnp.dot(act, w, preferred_element_type=jnp.float32)
    for p in range(out_ref.shape[0]):
        for b in range(4):
            part = sums[b][p * 2 : (p + 1) * 2].astype(jnp.bfloat16)
            out_ref[p, :, b * 256 : (b + 1) * 256] = part


def last_kernel(place_ref, landed_ref, stream_ref, out_ref):
    core = place_ref[2]
    for g in range(4):
        total = landed_ref[g * 16].astype(jnp.float32)
        for z in range(1, 16):
            total += landed_ref[g * 16 + z].astype(jnp.float32)
        for b in range(8):
            of = core if b < 4 else 1 - core
            x = (g // 2) * 2 + place_ref[0]
            y = (g % 2) * 2 + place_ref[1]
            if b & 1:
                x = lax.rem(x + 1 + 2 * of, 4)
            if b & 2:
                y = lax.rem(y + 1 + 2 * of, 4)
            at = pl.ds(pl.multiple_of(x * 1024 + y * 256 + of * HEAD, HEAD), HEAD)
            mixture = total[:, b * HEAD : (b + 1) * HEAD]
            out_ref[:, at] = (stream_ref[:, at] + mixture).astype(jnp.bfloat16)


def in_hbm(a):
    return pltpu.with_memory_space_constraint(a, pltpu.HBM)


def tie(first, a):
    return lax.optimization_barrier((first, a))[1]


def exchange(a, axes):
    return lax.all_to_all(a, axes, split_axis=0, concat_axis=0, tiled=True)


def pick_table(expert_ids, gate_wts, owners):
    wanted = jnp.arange(owners * LOCAL).reshape(owners, 1, LOCAL, 1)
    hit = expert_ids[None, :, None, :] == wanted
    gates = jnp.sum(jnp.where(hit, gate_wts[None, :, None, :], 0.0), axis=-1)
    high = gates.astype(jnp.bfloat16)
    rest = (gates - high.astype(jnp.float32)).astype(jnp.bfloat16)
    second = jnp.any(hit[:, 1], axis=-1).astype(jnp.bfloat16)
    line = jnp.concatenate([high.reshape(owners, 8), rest.reshape(owners, 8), second], axis=1)
    return jnp.pad(line, ((0, 0), (0, 108)))


def on_device(
    queries,
    fresh_key_value,
    resid,
    norm_gain,
    res_cache,
    res_len,
    long_cache,
    long_len,
    migrate_from,
    expert_ids,
    gate_wts,
    w_gate,
    w_up,
    w_down,
):
    bf16, f32 = jnp.bfloat16, jnp.float32
    core = lax.axis_index("c").reshape(1)
    place = jnp.stack([lax.axis_index(a) for a in ("xl", "yl", "c")])
    expert = lax.axis_index(Z).reshape(1)
    me = lax.axis_index(PLANE).reshape(1)
    owners = 16
    swap = lambda a: lax.ppermute(a, "c", [(0, 1), (1, 0)])

    ask, mine = pl.pallas_call(
        ask_kernel,
        out_shape=(
            jax.ShapeDtypeStruct((32, 48, HEAD), bf16),
            jax.ShapeDtypeStruct((48, HEAD), bf16),
        ),
        in_specs=[VMEM, VMEM],
        out_specs=(VMEM, VMEM),
        scratch_shapes=[pltpu.VMEM((2, 48, HEAD), f32)],
        compiler_params=params(4),
        name="ask",
    )(in_hbm(queries), in_hbm(fresh_key_value))
    asked = exchange(ask, PLANE)

    own = pl.pallas_call(
        resident_kernel,
        out_shape=jax.ShapeDtypeStruct((HEADS, HEAD), bf16),
        in_specs=[SMEM, VMEM, VMEM],
        out_specs=VMEM,
        compiler_params=params(4),
        name="resident_attention",
    )(res_len, mine, res_cache[0])
    onward = [(i * 2 + c, ((i + 3 + 2 * c) % 4) * 2 + c) for i in range(4) for c in range(2)]
    far = [
        (i * 8 + t, (onward[2 * i + t % 2][1] // 2) * 8 + u) for i in range(4) for t, u in onward
    ]
    source = migrate_from.reshape(32)
    guest = pl.pallas_call(
        guest_kernel,
        out_shape=jax.ShapeDtypeStruct((32, HEADS, HEAD), bf16),
        in_specs=[SMEM, SMEM, SMEM, VMEM, VMEM],
        out_specs=VMEM,
        compiler_params=params(8),
        name="guest_attention",
    )(me, in_hbm(source), in_hbm(long_len.reshape(32)), asked, in_hbm(long_cache[0]))
    back = exchange(guest, PLANE)
    meta = pick_table(expert_ids, gate_wts, owners)
    attn, stream, tokens = pl.pallas_call(
        token_kernel,
        out_shape=(
            jax.ShapeDtypeStruct((2, HEADS, HEAD), bf16),
            jax.ShapeDtypeStruct((2, HEADS, HEAD), f32),
            jax.ShapeDtypeStruct((owners, 80, HEAD), bf16),
        ),
        in_specs=[SMEM, SMEM] + [VMEM] * 5,
        out_specs=(VMEM, VMEM, VMEM),
        compiler_params=params(8),
        name="tokens",
    )(me, source, own, back, resid.reshape(2, HEADS, HEAD), norm_gain.reshape(HEADS, HEAD), meta)
    later = tie(stream, w_down)
    by_both = lax.ppermute(later, PLANE, far)
    by_x = lax.ppermute(later, X + ("c",), onward)
    by_y = [lax.ppermute(a, Y + ("c",), onward) for a in (later[:2], later[2:])]

    arrived = exchange(tokens, ("zl", "zh"))
    chosen = pl.pallas_call(
        select_kernel,
        out_shape=jax.ShapeDtypeStruct((16, owners, D + HEAD), bf16),
        in_specs=[SMEM, VMEM, VMEM],
        out_specs=VMEM,
        compiler_params=params(12),
        name="select_rows",
    )(expert, arrived[:, :64].reshape(owners, 2 * D), arrived[:, 64:])
    chosen, by_both, by_x, by_y = lax.optimization_barrier((chosen, by_both, by_x, by_y))
    gate_b, up_b = swap(w_gate), swap(w_up)
    downs = [w_down, by_x, by_both] + by_y
    downs += [swap(a) for a in downs]
    chosen = exchange(chosen, XY).reshape(16 * owners, D + HEAD)
    hidden, gates = pl.pallas_call(
        up_kernel,
        out_shape=(
            jax.ShapeDtypeStruct((16, 64, 2 * UNITS), bf16),
            jax.ShapeDtypeStruct((4, 64, HEAD), bf16),
        ),
        in_specs=[SMEM, VMEM] + [HBM] * 4,
        out_specs=(VMEM, VMEM),
        scratch_shapes=[pltpu.VMEM((4 * UNITS, D), bf16), pltpu.SemaphoreType.DMA((4,))],
        compiler_params=params(20),
        name="gate_up",
    )(core, chosen, *[in_hbm(a) for a in (w_gate, w_up, gate_b, up_b)])
    hidden = exchange(hidden, XY)
    partial = pl.pallas_call(
        down_kernel,
        out_shape=jax.ShapeDtypeStruct((64, 2, 8 * HEAD), bf16),
        in_specs=[SMEM, VMEM, VMEM] + [HBM] * 10,
        out_specs=VMEM,
        scratch_shapes=[
            pltpu.VMEM((LOCAL, 8, FFW, HEAD), bf16),
            pltpu.SemaphoreType.DMA((LOCAL, 8)),
        ],
        compiler_params=params(24),
        name="down",
    )(place, hidden, gates, *[in_hbm(a) for a in downs])
    landed = exchange(partial, ("xh", "yh", "zl", "zh"))
    layer_out = pl.pallas_call(
        last_kernel,
        out_shape=jax.ShapeDtypeStruct((2, D), bf16),
        in_specs=[SMEM, VMEM, VMEM],
        out_specs=VMEM,
        compiler_params=params(4),
        name="layer_out",
    )(place, landed, stream.reshape(2, D))
    return attn.reshape(2, D), layer_out


def solution(mesh):
    fine = Mesh(mesh.devices.reshape(2, 2, 2, 2, 2, 4, 4), ALL)
    rows, experts = P(ALL, None), P(Z + PLANE, None)
    cache = P(ALL, None, None)
    placed = (
        rows,
        rows,
        rows,
        P(),
        cache,
        P(ALL),
        cache,
        P(None, Z),
        P(None, Z),
        rows,
        rows,
        experts,
        experts,
        P(Z, None, PLANE),
    )
    return jax.shard_map(
        on_device, mesh=fine, in_specs=placed, out_specs=(rows, rows), check_vma=False
    )
```

```python
import functools
import math

import jax
import jax.numpy as jnp
from jax import lax
from jax.experimental import pallas as pl
from jax.experimental.pallas import tpu as pltpu
from jax.sharding import Mesh
from jax.sharding import PartitionSpec as P

HEADS = 32
GROUP = 16
HEAD = 128
D = 4096
FFW = 1536
LOCAL = 4
UNITS = 192
X = ("xh", "xl")
Y = ("yh", "yl")
XY = X + Y
PLANE = XY + ("c",)
Z = ("zh", "zl")
ALL = PLANE + Z
VMEM = pl.BlockSpec(memory_space=pltpu.VMEM)
SMEM = pl.BlockSpec(memory_space=pltpu.SMEM)
HBM = pl.BlockSpec(memory_space=pltpu.HBM)


def params(mib):
    return pltpu.CompilerParams(vmem_limit_bytes=mib << 20)


def attend(q, cache_ref, fresh, length):
    slots = cache_ref.shape[0]
    fresh = fresh.astype(jnp.float32)
    outs = []
    for g in range(2):
        qg = q[g * GROUP : (g + 1) * GROUP]
        keys = cache_ref[:, g * HEAD : (g + 1) * HEAD]
        values = cache_ref[:, (2 + g) * HEAD : (3 + g) * HEAD]
        scale = 1.0 / math.sqrt(HEAD)
        scores = lax.dot_general(
            qg, keys, (((1,), (1,)), ((), ())), preferred_element_type=jnp.float32
        )
        scores = scores * scale
        live = lax.broadcasted_iota(jnp.int32, (GROUP, slots), 1) < length
        scores = jnp.where(live, scores, -1e30)
        last = (
            jnp.sum(qg.astype(jnp.float32) * fresh[g : g + 1], axis=1, keepdims=True)
            * scale
        )
        peak = jnp.maximum(jnp.max(scores, axis=1, keepdims=True), last)
        weights = jnp.where(live, jnp.exp(scores - peak), 0.0).astype(jnp.bfloat16)
        end = jnp.exp(last - peak).astype(jnp.bfloat16).astype(jnp.float32)
        total = jnp.sum(weights.astype(jnp.float32), axis=1, keepdims=True) + end
        summed = jnp.dot(weights, values, preferred_element_type=jnp.float32)
        summed = summed + end * fresh[2 + g : 3 + g]
        outs.append(summed / total)
    return jnp.concatenate(outs, axis=0)


def ask_kernel(q_ref, kv_ref, ask_ref, own_ref, line_ref):
    q = q_ref[...].astype(jnp.float32)
    kv = kv_ref[...].astype(jnp.float32)
    line_ref[...] = jnp.zeros(line_ref.shape, jnp.float32)
    for r in range(2):
        for h in range(HEADS):
            line_ref[r, h : h + 1] = q[r : r + 1, h * HEAD : (h + 1) * HEAD]
        for h in range(4):
            line_ref[r, 32 + h : 33 + h] = kv[r : r + 1, h * HEAD : (h + 1) * HEAD]
    own_ref[...] = line_ref[0].astype(jnp.bfloat16)
    ask = line_ref[1].astype(jnp.bfloat16)
    for p in range(ask_ref.shape[0]):
        ask_ref[p] = ask


def resident_kernel(len_ref, own_ref, cache_ref, out_ref):
    own = own_ref[...]
    out = attend(own[:32], cache_ref, own[32:48][:4], len_ref[0])
    out_ref[...] = out.astype(jnp.bfloat16)


def guest_kernel(me_ref, from_ref, len_ref, asked_ref, cache_ref, out_ref):
    me = me_ref[0]

    def look(i, found):
        return jnp.where(from_ref[i] == me, i, found)

    target = lax.fori_loop(0, from_ref.shape[0], look, 0)
    asked = asked_ref[target]
    out = attend(asked[:32], cache_ref, asked[32:48][:4], len_ref[me])
    out = out.astype(jnp.bfloat16)
    for r in range(out_ref.shape[0]):
        out_ref[r] = out


def token_kernel(
    me_ref, from_ref, own_ref, back_ref, resid_ref, gain_ref, meta_ref, attn_ref, stream_ref, out_ref, line_ref
):
    root = from_ref[me_ref[0]]
    rows = (own_ref[...], back_ref[root])
    for r in range(2):
        attn = rows[r].astype(jnp.float32)
        stream = resid_ref[r].astype(jnp.float32) + attn
        for h in range(HEADS):
            at = slice(h * HEAD, (h + 1) * HEAD)
            line_ref[r : r + 1, at] = attn[h : h + 1]
            stream_ref[r : r + 1, at] = stream[h : h + 1]
        square = jnp.sum(jnp.sum(stream * stream, axis=1, keepdims=True), axis=0, keepdims=True)
        normed = (stream * lax.rsqrt(square / D + 1e-06) * gain_ref[...]).astype(jnp.bfloat16)
        for e in range(out_ref.shape[0]):
            out_ref[e, r * 32 : (r + 1) * 32] = normed
    for e in range(out_ref.shape[0]):
        out_ref[e, 64:80] = meta_ref[...]
    attn_ref[...] = line_ref[...].astype(jnp.bfloat16)


def select_kernel(expert_ref, rows_ref, meta_ref, out_ref):
    meta = meta_ref[...].astype(jnp.float32)
    mine = lax.broadcasted_iota(jnp.int32, meta.shape, 1) == expert_ref[0]
    meta = jnp.sum(jnp.where(mine, meta, 0.0), axis=1)
    line = meta.astype(jnp.bfloat16)
    first = rows_ref[:, :D].astype(jnp.float32)
    second = rows_ref[:, D:].astype(jnp.float32)
    for x in range(LOCAL):
        pick = meta[:, 16 + x : 17 + x] > 0.5
        row = jnp.where(pick, second, first).astype(jnp.bfloat16)
        for y in range(4):
            out_ref[x * 4 + y, :, :D] = row
            out_ref[x * 4 + y, :, D:] = line


def up_kernel(
    core_ref, rows_ref, ga_ref, ua_ref, gb_ref, ub_ref, out_ref, gate_ref, held_ref, sems
):
    copies = [
        pltpu.make_async_copy(w_ref, held_ref.at[pl.ds(i * UNITS, UNITS)], sems.at[i])
        for i, w_ref in enumerate((ga_ref, ua_ref, gb_ref, ub_ref))
    ]
    for copy in copies:
        copy.start()
    for copy in copies:
        copy.wait()
    dims = (((1,), (1,)), ((), ()))
    total = lax.dot_general(
        rows_ref[:, :D], held_ref[...], dims, preferred_element_type=jnp.float32
    )
    parts = [total[:, i * UNITS : (i + 1) * UNITS] for i in range(4)]
    acts = [
        gate * (1.0 / (1.0 + jnp.exp(-gate))) * up
        for gate, up in (parts[:2], parts[2:])
    ]
    both = jnp.where(
        core_ref[0] == 0,
        jnp.concatenate(acts, axis=1),
        jnp.concatenate(acts[::-1], axis=1),
    ).astype(jnp.bfloat16)
    for x in range(4):
        for y in range(4):
            there = slice((x * 4 + y) * 16, (x * 4 + y + 1) * 16)
            here = slice((x // 2 * 2 + y // 2) * 16, (x // 2 * 2 + y // 2 + 1) * 16)
            gate_ref[x % 2 * 2 + y % 2, here] = rows_ref[there, D:]
            for to_x in (x % 2, x % 2 + 2):
                for to_y in (y % 2, y % 2 + 2):
                    out_ref[to_x * 4 + to_y, here] = both[there]


def down_kernel(place_ref, act_ref, gate_ref, *refs):
    w_refs, (out_ref, held_ref, sems) = refs[:10], refs[10:]
    copies = []
    for x in range(LOCAL):
        sources = []
        for c in range(2):
            own, by_x, by_y, *by_both = w_refs[5 * c : 5 * c + 5]
            sources += [own.at[x], by_x.at[x], by_y.at[x], by_both[x // 2].at[x % 2]]
        copies.append(
            [
                pltpu.make_async_copy(source, held_ref.at[x, i], sems.at[x, i])
                for i, source in enumerate(sources)
            ]
        )
        for copy in copies[-1]:
            copy.start()
    n = act_ref.shape[1]
    row = lax.broadcasted_iota(jnp.int32, (2 * n, n), 0)
    slot = lax.broadcasted_iota(jnp.int32, (2 * n, n), 1)
    twice = jnp.where(row // 2 == slot, 1.0, 0.0).astype(jnp.bfloat16)
    gates = gate_ref[place_ref[0] * 2 + place_ref[1]]
    gates = jnp.dot(twice, gates, preferred_element_type=jnp.float32)
    lane = lax.broadcasted_iota(jnp.int32, gates.shape, 1)
    second = lax.broadcasted_iota(jnp.int32, gates.shape, 0) % 2
    sums = [0.0] * 4
    for x in range(LOCAL):
        act = jnp.concatenate([act_ref[x * 4 + y] for y in range(4)], axis=1)
        act = jnp.dot(twice, act, preferred_element_type=jnp.float32).astype(jnp.bfloat16)
        at = second * LOCAL + x
        weight = jnp.sum(
            jnp.where((lane == at) | (lane == at + 8), gates, 0.0), axis=1, keepdims=True
        )
        for copy in copies[x]:
            copy.wait()
        for b in range(4):
            w = jnp.concatenate([held_ref[x, 2 * b], held_ref[x, 2 * b + 1]], axis=1)
            sums[b] += weight * jnp.dot(act, w, preferred_element_type=jnp.float32)
    for p in range(out_ref.shape[0]):
        for b in range(4):
            part = sums[b][p * 2 : (p + 1) * 2].astype(jnp.bfloat16)
            out_ref[p, :, b * 256 : (b + 1) * 256] = part


def last_kernel(place_ref, landed_ref, stream_ref, out_ref):
    core = place_ref[2]
    for g in range(4):
        total = landed_ref[g * 16].astype(jnp.float32)
        for z in range(1, 16):
            total += landed_ref[g * 16 + z].astype(jnp.float32)
        for b in range(8):
            of = core if b < 4 else 1 - core
            x = (g // 2) * 2 + place_ref[0]
            y = (g % 2) * 2 + place_ref[1]
            if b & 1:
                x = lax.rem(x + 1 + 2 * of, 4)
            if b & 2:
                y = lax.rem(y + 1 + 2 * of, 4)
            at = pl.ds(pl.multiple_of(x * 1024 + y * 256 + of * HEAD, HEAD), HEAD)
            mixture = total[:, b * HEAD : (b + 1) * HEAD]
            out_ref[:, at] = (stream_ref[:, at] + mixture).astype(jnp.bfloat16)


def in_hbm(a):
    return pltpu.with_memory_space_constraint(a, pltpu.HBM)


def tie(first, a):
    return lax.optimization_barrier((first, a))[1]


def exchange(a, axes):
    return lax.all_to_all(a, axes, split_axis=0, concat_axis=0, tiled=True)


def pick_table(expert_ids, gate_wts, owners):
    wanted = jnp.arange(owners * LOCAL).reshape(owners, 1, LOCAL, 1)
    hit = expert_ids[None, :, None, :] == wanted
    gates = jnp.sum(jnp.where(hit, gate_wts[None, :, None, :], 0.0), axis=-1)
    high = gates.astype(jnp.bfloat16)
    rest = (gates - high.astype(jnp.float32)).astype(jnp.bfloat16)
    second = jnp.any(hit[:, 1], axis=-1).astype(jnp.bfloat16)
    line = jnp.concatenate([high.reshape(owners, 8), rest.reshape(owners, 8), second], axis=1)
    return jnp.pad(line, ((0, 0), (0, 108)))


def on_device(
    queries,
    fresh_key_value,
    resid,
    norm_gain,
    res_cache,
    res_len,
    long_cache,
    long_len,
    migrate_from,
    expert_ids,
    gate_wts,
    w_gate,
    w_up,
    w_down,
):
    bf16, f32 = jnp.bfloat16, jnp.float32
    core = lax.axis_index("c").reshape(1)
    place = jnp.stack([lax.axis_index(a) for a in ("xl", "yl", "c")])
    expert = lax.axis_index(Z).reshape(1)
    me = lax.axis_index(PLANE).reshape(1)
    owners = 16
    swap = lambda a: lax.ppermute(a, "c", [(0, 1), (1, 0)])

    ask, mine = pl.pallas_call(
        ask_kernel,
        out_shape=(
            jax.ShapeDtypeStruct((32, 48, HEAD), bf16),
            jax.ShapeDtypeStruct((48, HEAD), bf16),
        ),
        in_specs=[VMEM, VMEM],
        out_specs=(VMEM, VMEM),
        scratch_shapes=[pltpu.VMEM((2, 48, HEAD), f32)],
        compiler_params=params(4),
        name="ask",
    )(in_hbm(queries), in_hbm(fresh_key_value))
    asked = exchange(ask, PLANE)

    own = pl.pallas_call(
        resident_kernel,
        out_shape=jax.ShapeDtypeStruct((HEADS, HEAD), bf16),
        in_specs=[SMEM, VMEM, VMEM],
        out_specs=VMEM,
        compiler_params=params(4),
        name="resident_attention",
    )(res_len, mine, res_cache[0])
    onward = [(i * 2 + c, ((i + 3 + 2 * c) % 4) * 2 + c) for i in range(4) for c in range(2)]
    far = [
        (i * 8 + t, (onward[2 * i + t % 2][1] // 2) * 8 + u) for i in range(4) for t, u in onward
    ]
    source = migrate_from.reshape(32)
    guest = pl.pallas_call(
        guest_kernel,
        out_shape=jax.ShapeDtypeStruct((32, HEADS, HEAD), bf16),
        in_specs=[SMEM, SMEM, SMEM, VMEM, VMEM],
        out_specs=VMEM,
        compiler_params=params(8),
        name="guest_attention",
    )(me, in_hbm(source), in_hbm(long_len.reshape(32)), asked, in_hbm(long_cache[0]))
    back = exchange(guest, PLANE)
    meta = pick_table(expert_ids, gate_wts, owners)
    attn, stream, tokens = pl.pallas_call(
        token_kernel,
        out_shape=(
            jax.ShapeDtypeStruct((2, D), bf16),
            jax.ShapeDtypeStruct((2, D), f32),
            jax.ShapeDtypeStruct((owners, 80, HEAD), bf16),
        ),
        in_specs=[SMEM, SMEM] + [VMEM] * 5,
        out_specs=(VMEM, VMEM, VMEM),
        scratch_shapes=[pltpu.VMEM((2, D), f32)],
        compiler_params=params(8),
        name="tokens",
    )(me, source, own, back, resid.reshape(2, HEADS, HEAD), norm_gain.reshape(HEADS, HEAD), meta)
    later = tie(stream, w_down)
    by_x = lax.ppermute(later, X + ("c",), onward)
    by_y = lax.ppermute(later, Y + ("c",), onward)
    by_both = [lax.ppermute(a, PLANE, far) for a in (later[:2], later[2:])]

    arrived = exchange(tokens, ("zl", "zh"))
    chosen = pl.pallas_call(
        select_kernel,
        out_shape=jax.ShapeDtypeStruct((16, owners, D + HEAD), bf16),
        in_specs=[SMEM, VMEM, VMEM],
        out_specs=VMEM,
        compiler_params=params(12),
        name="select_rows",
    )(expert, arrived[:, :64].reshape(owners, 2 * D), arrived[:, 64:])
    chosen, by_both, by_x, by_y = lax.optimization_barrier((chosen, by_both, by_x, by_y))
    gate_b, up_b = swap(w_gate), swap(w_up)
    downs = [w_down, by_x, by_y] + by_both
    downs += [swap(a) for a in downs]
    chosen = exchange(chosen, XY).reshape(16 * owners, D + HEAD)
    hidden, gates = pl.pallas_call(
        up_kernel,
        out_shape=(
            jax.ShapeDtypeStruct((16, 64, 2 * UNITS), bf16),
            jax.ShapeDtypeStruct((4, 64, HEAD), bf16),
        ),
        in_specs=[SMEM, VMEM] + [HBM] * 4,
        out_specs=(VMEM, VMEM),
        scratch_shapes=[pltpu.VMEM((4 * UNITS, D), bf16), pltpu.SemaphoreType.DMA((4,))],
        compiler_params=params(20),
        name="gate_up",
    )(core, chosen, *[in_hbm(a) for a in (w_gate, w_up, gate_b, up_b)])
    hidden = exchange(hidden, XY)
    partial = pl.pallas_call(
        down_kernel,
        out_shape=jax.ShapeDtypeStruct((64, 2, 8 * HEAD), bf16),
        in_specs=[SMEM, VMEM, VMEM] + [HBM] * 10,
        out_specs=VMEM,
        scratch_shapes=[
            pltpu.VMEM((LOCAL, 8, FFW, HEAD), bf16),
            pltpu.SemaphoreType.DMA((LOCAL, 8)),
        ],
        compiler_params=params(24),
        name="down",
    )(place, hidden, gates, *[in_hbm(a) for a in downs])
    landed = exchange(partial, ("xh", "yh", "zl", "zh"))
    layer_out = pl.pallas_call(
        last_kernel,
        out_shape=jax.ShapeDtypeStruct((2, D), bf16),
        in_specs=[SMEM, VMEM, VMEM],
        out_specs=VMEM,
        compiler_params=params(4),
        name="layer_out",
    )(place, landed, stream)
    return attn, layer_out


def solution(mesh):
    fine = Mesh(mesh.devices.reshape(2, 2, 2, 2, 2, 4, 4), ALL)
    rows, experts = P(ALL, None), P(Z + PLANE, None)
    cache = P(ALL, None, None)
    placed = (
        rows,
        rows,
        rows,
        P(),
        cache,
        P(ALL),
        cache,
        P(None, Z),
        P(None, Z),
        rows,
        rows,
        experts,
        experts,
        P(Z, None, PLANE),
    )
    return jax.shard_map(
        on_device, mesh=fine, in_specs=placed, out_specs=(rows, rows), check_vma=False
    )
```

```python
import functools
import math

import jax
import jax.numpy as jnp
from jax import lax
from jax.experimental import pallas as pl
from jax.experimental.pallas import tpu as pltpu
from jax.sharding import Mesh
from jax.sharding import PartitionSpec as P

HEADS = 32
GROUP = 16
HEAD = 128
D = 4096
FFW = 1536
LOCAL = 4
UNITS = 192
X = ("xh", "xl")
Y = ("yh", "yl")
XY = X + Y
PLANE = XY + ("c",)
Z = ("zh", "zl")
ALL = PLANE + Z
VMEM = pl.BlockSpec(memory_space=pltpu.VMEM)
SMEM = pl.BlockSpec(memory_space=pltpu.SMEM)
HBM = pl.BlockSpec(memory_space=pltpu.HBM)


def params(mib):
    return pltpu.CompilerParams(vmem_limit_bytes=mib << 20)


def attend(q, cache_ref, fresh, length):
    slots = cache_ref.shape[0]
    fresh = fresh.astype(jnp.float32)
    outs = []
    for g in range(2):
        qg = q[g * GROUP : (g + 1) * GROUP]
        keys = cache_ref[:, g * HEAD : (g + 1) * HEAD]
        values = cache_ref[:, (2 + g) * HEAD : (3 + g) * HEAD]
        scale = 1.0 / math.sqrt(HEAD)
        scores = lax.dot_general(
            qg, keys, (((1,), (1,)), ((), ())), preferred_element_type=jnp.float32
        )
        scores = scores * scale
        live = lax.broadcasted_iota(jnp.int32, (GROUP, slots), 1) < length
        scores = jnp.where(live, scores, -1e30)
        last = (
            jnp.sum(qg.astype(jnp.float32) * fresh[g : g + 1], axis=1, keepdims=True)
            * scale
        )
        peak = jnp.maximum(jnp.max(scores, axis=1, keepdims=True), last)
        weights = jnp.where(live, jnp.exp(scores - peak), 0.0).astype(jnp.bfloat16)
        end = jnp.exp(last - peak).astype(jnp.bfloat16).astype(jnp.float32)
        total = jnp.sum(weights.astype(jnp.float32), axis=1, keepdims=True) + end
        summed = jnp.dot(weights, values, preferred_element_type=jnp.float32)
        summed = summed + end * fresh[2 + g : 3 + g]
        outs.append(summed / total)
    return jnp.concatenate(outs, axis=0)


def ask_kernel(q_ref, kv_ref, ask_ref, own_ref, line_ref):
    q = q_ref[...].astype(jnp.float32)
    kv = kv_ref[...].astype(jnp.float32)
    line_ref[...] = jnp.zeros(line_ref.shape, jnp.float32)
    for r in range(2):
        for h in range(HEADS):
            line_ref[r, h : h + 1] = q[r : r + 1, h * HEAD : (h + 1) * HEAD]
        for h in range(4):
            line_ref[r, 32 + h : 33 + h] = kv[r : r + 1, h * HEAD : (h + 1) * HEAD]
    own_ref[...] = line_ref[0].astype(jnp.bfloat16)
    ask = line_ref[1].astype(jnp.bfloat16)
    for p in range(ask_ref.shape[0]):
        ask_ref[p] = ask


def resident_kernel(len_ref, own_ref, cache_ref, out_ref):
    own = own_ref[...]
    out = attend(own[:32], cache_ref, own[32:48][:4], len_ref[0])
    out_ref[...] = out.astype(jnp.bfloat16)


def guest_kernel(me_ref, from_ref, len_ref, asked_ref, cache_ref, out_ref):
    me = me_ref[0]

    def look(i, found):
        return jnp.where(from_ref[i] == me, i, found)

    target = lax.fori_loop(0, from_ref.shape[0], look, 0)
    asked = asked_ref[target]
    out = attend(asked[:32], cache_ref, asked[32:48][:4], len_ref[me])
    out = out.astype(jnp.bfloat16)
    for r in range(out_ref.shape[0]):
        out_ref[r] = out


def token_kernel(
    me_ref, from_ref, own_ref, back_ref, resid_ref, gain_ref, meta_ref, attn_ref, stream_ref, out_ref, line_ref
):
    root = from_ref[me_ref[0]]
    rows = (own_ref[...], back_ref[root])
    for r in range(2):
        attn = rows[r].astype(jnp.float32)
        stream = resid_ref[r].astype(jnp.float32) + attn
        for h in range(HEADS):
            at = slice(h * HEAD, (h + 1) * HEAD)
            line_ref[r : r + 1, at] = attn[h : h + 1]
            stream_ref[r : r + 1, at] = stream[h : h + 1]
        square = jnp.sum(jnp.sum(stream * stream, axis=1, keepdims=True), axis=0, keepdims=True)
        normed = (stream * lax.rsqrt(square / D + 1e-06) * gain_ref[...]).astype(jnp.bfloat16)
        out_ref[r * 32 : (r + 1) * 32] = normed
    out_ref[64:80] = meta_ref[...]
    attn_ref[...] = line_ref[...].astype(jnp.bfloat16)


def select_kernel(expert_ref, rows_ref, meta_ref, out_ref, line_ref):
    meta = meta_ref[...].astype(jnp.float32)
    mine = lax.broadcasted_iota(jnp.int32, meta.shape, 1) == expert_ref[0]
    meta = jnp.sum(jnp.where(mine, meta, 0.0), axis=1)
    line_ref[...] = meta
    first = rows_ref[:, :D].astype(jnp.float32)
    second = rows_ref[:, D:].astype(jnp.float32)
    for x in range(LOCAL):
        pick = meta[:, 16 + x : 17 + x] > 0.5
        row = jnp.where(pick, second, first).astype(jnp.bfloat16)
        for y in range(4):
            out_ref[x * 4 + y] = row


def expert_kernel(core_ref, rows_ref, *refs):
    w_refs, (out_ref, held_ref, down_ref, sems) = refs[:6], refs[6:]
    copies = [
        pltpu.make_async_copy(w_refs[i], held_ref.at[pl.ds(i * UNITS, UNITS)], sems.at[i])
        for i in range(4)
    ]
    copies += [
        pltpu.make_async_copy(w_refs[4 + i], down_ref.at[i], sems.at[4 + i]) for i in range(2)
    ]
    for copy in copies:
        copy.start()
    for copy in copies[:4]:
        copy.wait()
    dims = (((1,), (1,)), ((), ()))
    total = lax.dot_general(
        rows_ref[...], held_ref[...], dims, preferred_element_type=jnp.float32
    )
    parts = [total[:, i * UNITS : (i + 1) * UNITS] for i in range(4)]
    acts = [
        gate * (1.0 / (1.0 + jnp.exp(-gate))) * up
        for gate, up in (parts[:2], parts[2:])
    ]
    both = jnp.where(
        core_ref[0] == 0,
        jnp.concatenate(acts, axis=1),
        jnp.concatenate(acts[::-1], axis=1),
    ).astype(jnp.bfloat16)
    for copy in copies[4:]:
        copy.wait()
    for b in range(16):
        w = jnp.concatenate([down_ref[0, b], down_ref[1, b]], axis=1)
        part = jnp.dot(both, w, preferred_element_type=jnp.float32).astype(jnp.bfloat16)
        for p in range(16):
            out_ref[p, :, b * 256 : (b + 1) * 256] = part[p * 16 : (p + 1) * 16]


def mix_kernel(line_ref, landed_ref, out_ref):
    row = lax.broadcasted_iota(jnp.int32, (32, 16), 0)
    slot = lax.broadcasted_iota(jnp.int32, (32, 16), 1)
    twice = jnp.where(row // 2 == slot, 1.0, 0.0)
    line = line_ref[...]
    second = lax.broadcasted_iota(jnp.int32, (32, 1), 0) % 2
    weights = []
    for x in range(LOCAL):
        both = []
        for r in range(2):
            j = r * LOCAL + x
            gate = line[:, j : j + 1] + line[:, 8 + j : 9 + j]
            gate = jnp.sum(jnp.where(row // 2 == slot, gate.reshape(1, 16), 0.0), axis=1)
            both.append(gate.reshape(32, 1))
        weights.append(jnp.where(second == 0, both[0], both[1]))
    twice = twice.astype(jnp.bfloat16)
    width = 512
    for k in range(D // width):
        at = slice(k * width, (k + 1) * width)
        mixed = 0.0
        for x in range(LOCAL):
            total = landed_ref[x * 4, :, at].astype(jnp.float32)
            for y in range(1, 4):
                total += landed_ref[x * 4 + y, :, at].astype(jnp.float32)
            total = jnp.dot(twice, total.astype(jnp.bfloat16), preferred_element_type=jnp.float32)
            mixed += weights[x] * total
        for z in range(16):
            out_ref[z, :, at] = mixed[2 * z : 2 * z + 2].astype(jnp.bfloat16)


def last_kernel(core_ref, landed_ref, stream_ref, out_ref):
    total = landed_ref[0].astype(jnp.float32)
    for z in range(1, 16):
        total += landed_ref[z].astype(jnp.float32)
    even = core_ref[0] == 0
    for b in range(16):
        at = slice(b * 256, (b + 1) * 256)
        mixture = total[:, at]
        turned = jnp.concatenate([mixture[:, HEAD:], mixture[:, :HEAD]], axis=1)
        mixture = jnp.where(even, mixture, turned)
        out_ref[:, at] = (stream_ref[:, at] + mixture).astype(jnp.bfloat16)


def in_hbm(a):
    return pltpu.with_memory_space_constraint(a, pltpu.HBM)


def tie(first, a):
    return lax.optimization_barrier((first, a))[1]


def exchange(a, axes):
    return lax.all_to_all(a, axes, split_axis=0, concat_axis=0, tiled=True)


def pick_table(expert_ids, gate_wts, owners):
    wanted = jnp.arange(owners * LOCAL).reshape(owners, 1, LOCAL, 1)
    hit = expert_ids[None, :, None, :] == wanted
    gates = jnp.sum(jnp.where(hit, gate_wts[None, :, None, :], 0.0), axis=-1)
    high = gates.astype(jnp.bfloat16)
    rest = (gates - high.astype(jnp.float32)).astype(jnp.bfloat16)
    second = jnp.any(hit[:, 1], axis=-1).astype(jnp.bfloat16)
    line = jnp.concatenate([high.reshape(owners, 8), rest.reshape(owners, 8), second], axis=1)
    return jnp.pad(line, ((0, 0), (0, 108)))


def on_device(
    queries,
    fresh_key_value,
    resid,
    norm_gain,
    res_cache,
    res_len,
    long_cache,
    long_len,
    migrate_from,
    expert_ids,
    gate_wts,
    w_gate,
    w_up,
    w_down,
):
    bf16, f32 = jnp.bfloat16, jnp.float32
    core = lax.axis_index("c").reshape(1)
    expert = lax.axis_index(Z).reshape(1)
    me = lax.axis_index(PLANE).reshape(1)
    owners = 16
    swap = lambda a: lax.ppermute(a, "c", [(0, 1), (1, 0)])

    ask, mine = pl.pallas_call(
        ask_kernel,
        out_shape=(
            jax.ShapeDtypeStruct((32, 48, HEAD), bf16),
            jax.ShapeDtypeStruct((48, HEAD), bf16),
        ),
        in_specs=[VMEM, VMEM],
        out_specs=(VMEM, VMEM),
        scratch_shapes=[pltpu.VMEM((2, 48, HEAD), f32)],
        compiler_params=params(4),
        name="ask",
    )(in_hbm(queries), in_hbm(fresh_key_value))
    asked = exchange(ask, PLANE)

    own = pl.pallas_call(
        resident_kernel,
        out_shape=jax.ShapeDtypeStruct((HEADS, HEAD), bf16),
        in_specs=[SMEM, VMEM, VMEM],
        out_specs=VMEM,
        compiler_params=params(4),
        name="resident_attention",
    )(res_len, mine, res_cache[0])
    source = migrate_from.reshape(32)
    guest = pl.pallas_call(
        guest_kernel,
        out_shape=jax.ShapeDtypeStruct((32, HEADS, HEAD), bf16),
        in_specs=[SMEM, SMEM, SMEM, VMEM, VMEM],
        out_specs=VMEM,
        compiler_params=params(8),
        name="guest_attention",
    )(me, in_hbm(source), in_hbm(long_len.reshape(32)), asked, in_hbm(long_cache[0]))
    back = exchange(guest, PLANE)
    meta = pick_table(expert_ids, gate_wts, owners)
    attn, stream, tokens = pl.pallas_call(
        token_kernel,
        out_shape=(
            jax.ShapeDtypeStruct((2, D), bf16),
            jax.ShapeDtypeStruct((2, D), f32),
            jax.ShapeDtypeStruct((80, HEAD), bf16),
        ),
        in_specs=[SMEM, SMEM] + [VMEM] * 5,
        out_specs=(VMEM, VMEM, VMEM),
        scratch_shapes=[pltpu.VMEM((2, D), f32)],
        compiler_params=params(8),
        name="tokens",
    )(me, source, own, back, resid.reshape(2, HEADS, HEAD), norm_gain.reshape(HEADS, HEAD), meta)
    down_a = exchange(tie(stream, w_down).reshape(16, 2 * UNITS, HEAD), XY)
    arrived = lax.all_gather(tokens, Z)
    chosen, line = pl.pallas_call(
        select_kernel,
        out_shape=(
            jax.ShapeDtypeStruct((16, owners, D), bf16),
            jax.ShapeDtypeStruct((owners, HEAD), f32),
        ),
        in_specs=[SMEM, VMEM, VMEM],
        out_specs=(VMEM, VMEM),
        compiler_params=params(12),
        name="select_rows",
    )(expert, arrived[:, :64].reshape(owners, 2 * D), arrived[:, 64:])
    chosen, down_a = lax.optimization_barrier((chosen, down_a))
    gate_b, up_b, down_b = swap(w_gate), swap(w_up), swap(down_a)
    chosen = exchange(chosen, XY).reshape(16 * owners, D)
    produced = pl.pallas_call(
        expert_kernel,
        out_shape=jax.ShapeDtypeStruct((16, owners, D), bf16),
        in_specs=[SMEM, VMEM] + [HBM] * 6,
        out_specs=VMEM,
        scratch_shapes=[
            pltpu.VMEM((4 * UNITS, D), bf16),
            pltpu.VMEM((2, 16, 2 * UNITS, HEAD), bf16),
            pltpu.SemaphoreType.DMA((6,)),
        ],
        compiler_params=params(28),
        name="experts",
    )(core, chosen, *[in_hbm(a) for a in (w_gate, w_up, gate_b, up_b, down_a, down_b)])
    mixed = pl.pallas_call(
        mix_kernel,
        out_shape=jax.ShapeDtypeStruct((owners, 2, D), bf16),
        in_specs=[VMEM, VMEM],
        out_specs=VMEM,
        compiler_params=params(8),
        name="mix",
    )(line, exchange(produced, XY))
    landed = exchange(mixed, Z)
    layer_out = pl.pallas_call(
        last_kernel,
        out_shape=jax.ShapeDtypeStruct((2, D), bf16),
        in_specs=[SMEM, VMEM, VMEM],
        out_specs=VMEM,
        compiler_params=params(4),
        name="layer_out",
    )(core, landed, stream)
    return attn, layer_out


def solution(mesh):
    fine = Mesh(mesh.devices.reshape(2, 2, 2, 2, 2, 4, 4), ALL)
    rows, experts = P(ALL, None), P(Z + PLANE, None)
    cache = P(ALL, None, None)
    placed = (
        rows,
        rows,
        rows,
        P(),
        cache,
        P(ALL),
        cache,
        P(None, Z),
        P(None, Z),
        rows,
        rows,
        experts,
        experts,
        P(Z, None, PLANE),
    )
    return jax.shard_map(
        on_device, mesh=fine, in_specs=placed, out_specs=(rows, rows), check_vma=False
    )
```

```python
import functools
import math

import jax
import jax.numpy as jnp
from jax import lax
from jax.experimental import pallas as pl
from jax.experimental.pallas import tpu as pltpu
from jax.sharding import Mesh
from jax.sharding import PartitionSpec as P

HEADS = 32
GROUP = 16
HEAD = 128
D = 4096
FFW = 1536
LOCAL = 4
UNITS = 192
X = ("xh", "xl")
Y = ("yh", "yl")
XY = X + Y
PLANE = XY + ("c",)
Z = ("zh", "zl")
ALL = PLANE + Z
VMEM = pl.BlockSpec(memory_space=pltpu.VMEM)
SMEM = pl.BlockSpec(memory_space=pltpu.SMEM)
HBM = pl.BlockSpec(memory_space=pltpu.HBM)


def params(mib):
    return pltpu.CompilerParams(vmem_limit_bytes=mib << 20)


def attend(q, cache_ref, fresh, length):
    slots = cache_ref.shape[0]
    fresh = fresh.astype(jnp.float32)
    outs = []
    for g in range(2):
        qg = q[g * GROUP : (g + 1) * GROUP]
        keys = cache_ref[:, g * HEAD : (g + 1) * HEAD]
        values = cache_ref[:, (2 + g) * HEAD : (3 + g) * HEAD]
        scale = 1.0 / math.sqrt(HEAD)
        scores = lax.dot_general(
            qg, keys, (((1,), (1,)), ((), ())), preferred_element_type=jnp.float32
        )
        scores = scores * scale
        live = lax.broadcasted_iota(jnp.int32, (GROUP, slots), 1) < length
        scores = jnp.where(live, scores, -1e30)
        last = (
            jnp.sum(qg.astype(jnp.float32) * fresh[g : g + 1], axis=1, keepdims=True)
            * scale
        )
        peak = jnp.maximum(jnp.max(scores, axis=1, keepdims=True), last)
        weights = jnp.where(live, jnp.exp(scores - peak), 0.0).astype(jnp.bfloat16)
        end = jnp.exp(last - peak).astype(jnp.bfloat16).astype(jnp.float32)
        total = jnp.sum(weights.astype(jnp.float32), axis=1, keepdims=True) + end
        summed = jnp.dot(weights, values, preferred_element_type=jnp.float32)
        summed = summed + end * fresh[2 + g : 3 + g]
        outs.append(summed / total)
    return jnp.concatenate(outs, axis=0)


def ask_kernel(q_ref, kv_ref, ask_ref, own_ref, line_ref):
    q = q_ref[...].astype(jnp.float32)
    kv = kv_ref[...].astype(jnp.float32)
    line_ref[...] = jnp.zeros(line_ref.shape, jnp.float32)
    for r in range(2):
        for h in range(HEADS):
            line_ref[r, h : h + 1] = q[r : r + 1, h * HEAD : (h + 1) * HEAD]
        for h in range(4):
            line_ref[r, 32 + h : 33 + h] = kv[r : r + 1, h * HEAD : (h + 1) * HEAD]
    own_ref[...] = line_ref[0].astype(jnp.bfloat16)
    ask = line_ref[1].astype(jnp.bfloat16)
    for p in range(ask_ref.shape[0]):
        ask_ref[p] = ask


def resident_kernel(len_ref, own_ref, cache_ref, long_ref, out_ref, held_ref):
    held_ref[...] = long_ref[...]
    own = own_ref[...]
    out = attend(own[:32], cache_ref, own[32:48][:4], len_ref[0])
    out_ref[...] = out.astype(jnp.bfloat16)


def guest_kernel(me_ref, from_ref, len_ref, asked_ref, cache_ref, out_ref):
    me = me_ref[0]

    def look(i, found):
        return jnp.where(from_ref[i] == me, i, found)

    target = lax.fori_loop(0, from_ref.shape[0], look, 0)
    asked = asked_ref[target]
    out = attend(asked[:32], cache_ref, asked[32:48][:4], len_ref[me])
    out = out.astype(jnp.bfloat16)
    for r in range(out_ref.shape[0]):
        out_ref[r] = out


def token_kernel(
    me_ref, from_ref, own_ref, back_ref, resid_ref, gain_ref, meta_ref, attn_ref, stream_ref, out_ref, line_ref
):
    root = from_ref[me_ref[0]]
    rows = (own_ref[...], back_ref[root])
    for r in range(2):
        attn = rows[r].astype(jnp.float32)
        stream = resid_ref[r].astype(jnp.float32) + attn
        for h in range(HEADS):
            at = slice(h * HEAD, (h + 1) * HEAD)
            line_ref[r : r + 1, at] = attn[h : h + 1]
            stream_ref[r : r + 1, at] = stream[h : h + 1]
        square = jnp.sum(jnp.sum(stream * stream, axis=1, keepdims=True), axis=0, keepdims=True)
        normed = (stream * lax.rsqrt(square / D + 1e-06) * gain_ref[...]).astype(jnp.bfloat16)
        out_ref[r * 32 : (r + 1) * 32] = normed
    out_ref[64:80] = meta_ref[...]
    attn_ref[...] = line_ref[...].astype(jnp.bfloat16)


def select_kernel(expert_ref, rows_ref, meta_ref, out_ref, line_ref):
    meta = meta_ref[...].astype(jnp.float32)
    mine = lax.broadcasted_iota(jnp.int32, meta.shape, 1) == expert_ref[0]
    meta = jnp.sum(jnp.where(mine, meta, 0.0), axis=1)
    line_ref[...] = meta
    first = rows_ref[:, :D].astype(jnp.float32)
    second = rows_ref[:, D:].astype(jnp.float32)
    for x in range(LOCAL):
        pick = meta[:, 16 + x : 17 + x] > 0.5
        row = jnp.where(pick, second, first).astype(jnp.bfloat16)
        for y in range(4):
            out_ref[y * 4 + x] = row


def expert_kernel(core_ref, rows_ref, *refs):
    w_refs, (out_ref, held_ref, down_ref, sems) = refs[:6], refs[6:]
    copies = [
        pltpu.make_async_copy(w_refs[i], held_ref.at[pl.ds(i * UNITS, UNITS)], sems.at[i])
        for i in range(4)
    ]
    copies += [
        pltpu.make_async_copy(w_refs[4 + i], down_ref.at[i], sems.at[4 + i]) for i in range(2)
    ]
    for copy in copies:
        copy.start()
    for copy in copies[:4]:
        copy.wait()
    dims = (((1,), (1,)), ((), ()))
    total = lax.dot_general(
        rows_ref[...], held_ref[...], dims, preferred_element_type=jnp.float32
    )
    parts = [total[:, i * UNITS : (i + 1) * UNITS] for i in range(4)]
    acts = [
        gate * (1.0 / (1.0 + jnp.exp(-gate))) * up
        for gate, up in (parts[:2], parts[2:])
    ]
    both = jnp.where(
        core_ref[0] == 0,
        jnp.concatenate(acts, axis=1),
        jnp.concatenate(acts[::-1], axis=1),
    ).astype(jnp.bfloat16)
    for copy in copies[4:]:
        copy.wait()
    for b in range(16):
        w = jnp.concatenate([down_ref[0, b], down_ref[1, b]], axis=1)
        part = jnp.dot(both, w, preferred_element_type=jnp.float32).astype(jnp.bfloat16)
        for p in range(16):
            out_ref[p, :, b * 256 : (b + 1) * 256] = part[p * 16 : (p + 1) * 16]


def mix_kernel(line_ref, landed_ref, out_ref):
    row = lax.broadcasted_iota(jnp.int32, (32, 16), 0)
    slot = lax.broadcasted_iota(jnp.int32, (32, 16), 1)
    twice = jnp.where(row // 2 == slot, 1.0, 0.0)
    line = line_ref[...]
    second = lax.broadcasted_iota(jnp.int32, (32, 1), 0) % 2
    weights = []
    for x in range(LOCAL):
        both = []
        for r in range(2):
            j = r * LOCAL + x
            gate = line[:, j : j + 1] + line[:, 8 + j : 9 + j]
            gate = jnp.sum(jnp.where(row // 2 == slot, gate.reshape(1, 16), 0.0), axis=1)
            both.append(gate.reshape(32, 1))
        weights.append(jnp.where(second == 0, both[0], both[1]))
    twice = twice.astype(jnp.bfloat16)
    width = 512
    for k in range(D // width):
        at = slice(k * width, (k + 1) * width)
        mixed = 0.0
        for x in range(LOCAL):
            total = landed_ref[x, :, at].astype(jnp.float32)
            for y in range(1, 4):
                total += landed_ref[y * 4 + x, :, at].astype(jnp.float32)
            total = jnp.dot(twice, total.astype(jnp.bfloat16), preferred_element_type=jnp.float32)
            mixed += weights[x] * total
        for z in range(16):
            out_ref[z, :, at] = mixed[2 * z : 2 * z + 2].astype(jnp.bfloat16)


def last_kernel(core_ref, landed_ref, stream_ref, out_ref):
    total = landed_ref[0].astype(jnp.float32)
    for z in range(1, 16):
        total += landed_ref[z].astype(jnp.float32)
    even = core_ref[0] == 0
    for b in range(16):
        at = slice(b * 256, (b + 1) * 256)
        mixture = total[:, at]
        turned = jnp.concatenate([mixture[:, HEAD:], mixture[:, :HEAD]], axis=1)
        mixture = jnp.where(even, mixture, turned)
        out_ref[:, at] = (stream_ref[:, at] + mixture).astype(jnp.bfloat16)


def in_hbm(a):
    return pltpu.with_memory_space_constraint(a, pltpu.HBM)


def tie(first, a):
    return lax.optimization_barrier((first, a))[1]


def exchange(a, axes):
    return lax.all_to_all(a, axes, split_axis=0, concat_axis=0, tiled=True)


def pick_table(expert_ids, gate_wts, owners):
    wanted = jnp.arange(owners * LOCAL).reshape(owners, 1, LOCAL, 1)
    hit = expert_ids[None, :, None, :] == wanted
    gates = jnp.sum(jnp.where(hit, gate_wts[None, :, None, :], 0.0), axis=-1)
    high = gates.astype(jnp.bfloat16)
    rest = (gates - high.astype(jnp.float32)).astype(jnp.bfloat16)
    second = jnp.any(hit[:, 1], axis=-1).astype(jnp.bfloat16)
    line = jnp.concatenate([high.reshape(owners, 8), rest.reshape(owners, 8), second], axis=1)
    return jnp.pad(line, ((0, 0), (0, 108)))


def on_device(
    queries,
    fresh_key_value,
    resid,
    norm_gain,
    res_cache,
    res_len,
    long_cache,
    long_len,
    migrate_from,
    expert_ids,
    gate_wts,
    w_gate,
    w_up,
    w_down,
):
    bf16, f32 = jnp.bfloat16, jnp.float32
    core = lax.axis_index("c").reshape(1)
    expert = lax.axis_index(Z).reshape(1)
    me = lax.axis_index(PLANE).reshape(1)
    owners = 16
    swap = lambda a: lax.ppermute(a, "c", [(0, 1), (1, 0)])

    ask, mine = pl.pallas_call(
        ask_kernel,
        out_shape=(
            jax.ShapeDtypeStruct((32, 48, HEAD), bf16),
            jax.ShapeDtypeStruct((48, HEAD), bf16),
        ),
        in_specs=[VMEM, VMEM],
        out_specs=(VMEM, VMEM),
        scratch_shapes=[pltpu.VMEM((2, 48, HEAD), f32)],
        compiler_params=params(4),
        name="ask",
    )(in_hbm(queries), in_hbm(fresh_key_value))
    asked = exchange(ask, PLANE)

    own, held_cache = pl.pallas_call(
        resident_kernel,
        out_shape=(
            jax.ShapeDtypeStruct((HEADS, HEAD), bf16),
            jax.ShapeDtypeStruct(long_cache.shape[1:], bf16),
        ),
        in_specs=[SMEM, VMEM, VMEM, VMEM],
        out_specs=(VMEM, VMEM),
        compiler_params=params(4),
        name="resident_attention",
    )(res_len, mine, res_cache[0], in_hbm(long_cache[0]))
    source = migrate_from.reshape(32)
    guest = pl.pallas_call(
        guest_kernel,
        out_shape=jax.ShapeDtypeStruct((32, HEADS, HEAD), bf16),
        in_specs=[SMEM, SMEM, SMEM, VMEM, VMEM],
        out_specs=VMEM,
        compiler_params=params(8),
        name="guest_attention",
    )(me, in_hbm(source), in_hbm(long_len.reshape(32)), asked, held_cache)
    back = exchange(guest, PLANE)
    meta = pick_table(expert_ids, gate_wts, owners)
    attn, stream, tokens = pl.pallas_call(
        token_kernel,
        out_shape=(
            jax.ShapeDtypeStruct((2, D), bf16),
            jax.ShapeDtypeStruct((2, D), f32),
            jax.ShapeDtypeStruct((80, HEAD), bf16),
        ),
        in_specs=[SMEM, SMEM] + [VMEM] * 5,
        out_specs=(VMEM, VMEM, VMEM),
        scratch_shapes=[pltpu.VMEM((2, D), f32)],
        compiler_params=params(8),
        name="tokens",
    )(me, source, own, back, resid.reshape(2, HEADS, HEAD), norm_gain.reshape(HEADS, HEAD), meta)
    down_a = exchange(tie(stream, w_down).reshape(16, 2 * UNITS, HEAD), XY)
    arrived = lax.all_gather(tokens, Z)
    chosen, line = pl.pallas_call(
        select_kernel,
        out_shape=(
            jax.ShapeDtypeStruct((16, owners, D), bf16),
            jax.ShapeDtypeStruct((owners, HEAD), f32),
        ),
        in_specs=[SMEM, VMEM, VMEM],
        out_specs=(VMEM, VMEM),
        compiler_params=params(12),
        name="select_rows",
    )(expert, arrived[:, :64].reshape(owners, 2 * D), arrived[:, 64:])
    chosen, down_a = lax.optimization_barrier((chosen, down_a))
    gate_b, up_b, down_b = swap(w_gate), swap(w_up), swap(down_a)
    chosen = exchange(chosen, Y + X).reshape(16 * owners, D)
    produced = pl.pallas_call(
        expert_kernel,
        out_shape=jax.ShapeDtypeStruct((16, owners, D), bf16),
        in_specs=[SMEM, VMEM] + [HBM] * 6,
        out_specs=VMEM,
        scratch_shapes=[
            pltpu.VMEM((4 * UNITS, D), bf16),
            pltpu.VMEM((2, 16, 2 * UNITS, HEAD), bf16),
            pltpu.SemaphoreType.DMA((6,)),
        ],
        compiler_params=params(28),
        name="experts",
    )(core, chosen, *[in_hbm(a) for a in (w_gate, w_up, gate_b, up_b, down_a, down_b)])
    mixed = pl.pallas_call(
        mix_kernel,
        out_shape=jax.ShapeDtypeStruct((owners, 2, D), bf16),
        in_specs=[VMEM, VMEM],
        out_specs=VMEM,
        compiler_params=params(8),
        name="mix",
    )(line, exchange(produced, Y + X))
    landed = exchange(mixed, Z)
    layer_out = pl.pallas_call(
        last_kernel,
        out_shape=jax.ShapeDtypeStruct((2, D), bf16),
        in_specs=[SMEM, VMEM, VMEM],
        out_specs=VMEM,
        compiler_params=params(4),
        name="layer_out",
    )(core, landed, stream)
    return attn, layer_out


def solution(mesh):
    fine = Mesh(mesh.devices.reshape(2, 2, 2, 2, 2, 4, 4), ALL)
    rows, experts = P(ALL, None), P(Z + PLANE, None)
    cache = P(ALL, None, None)
    placed = (
        rows,
        rows,
        rows,
        P(),
        cache,
        P(ALL),
        cache,
        P(None, Z),
        P(None, Z),
        rows,
        rows,
        experts,
        experts,
        P(Z, None, PLANE),
    )
    return jax.shard_map(
        on_device, mesh=fine, in_specs=placed, out_specs=(rows, rows), check_vma=False
    )
```
